32 devices in a mesh: pipe: 2 (over x), expert: 16 (over z, y, core).
Axes of the slice: x: 2, y: 2, z: 4, core: 2. Of those that a mesh axis runs over, the one named last changes fastest.
Arguments:
- x_first: bfloat16 [2, 2048, 4096], P('pipe', 'expert'), may hold values from -6 to 6
- grad_first: bfloat16 [2, 2048, 4096], P('pipe', 'expert'), may hold values from -12 to 12
- x_second: bfloat16 [2, 2048, 4096], P('pipe', 'expert'), may hold values from -6 to 6
- grad_last: bfloat16 [2048, 4096], P('expert'), may hold values from -12 to 12
- ids_first: int32 [2, 2048, 8], P('pipe', 'expert'), may hold values from 0 to 127, all different within a row; in each aligned block of 128 rows (0 to 127, 128 to 255, ..., all dimensions but the last counted through in order) at most 12 rows name the same one
- probs_first: float32 [2, 2048, 8], P('pipe', 'expert'), may hold values from 0.05 to 1
- ids_second: int32 [2, 2048, 8], P('pipe', 'expert'), may hold values from 0 to 127, all different within a row; in each aligned block of 128 rows (0 to 127, 128 to 255, ..., all dimensions but the last counted through in order) at most 12 rows name the same one
- probs_second: float32 [2, 2048, 8], P('pipe', 'expert'), may hold values from 0.05 to 1
- w_gate: bfloat16 [2, 16, 4096, 256], P('pipe', 'expert'), may hold values from -0.09375 to 0.09375
- w_up: bfloat16 [2, 16, 4096, 256], P('pipe', 'expert'), may hold values from -0.09375 to 0.09375
- w_down: bfloat16 [2, 16, 256, 4096], P('pipe', 'expert'), may hold values from -0.1875 to 0.1875
Outputs:
- dx_first: bfloat16 [2, 2048, 4096], P('pipe', 'expert')
- dx_second: bfloat16 [2, 2048, 4096], P('pipe', 'expert')
The draws below stay inside these ranges and needn't reach their ends.
Inputs may be any that keep to these rules, and one draw needn't show every extreme that they name: `ids_first`: each token names 8 different experts; among the rows of one device each expert is named by at most 12 tokens. `ids_second`: each token names 8 different experts; among the rows of one device each expert is named by at most 12 tokens.
All inputs are finite; a program needn't handle non-finite values.
Results may differ from the reference program's by a relative error of at most 0.006.
Values may be sent and summed in bfloat16 or wider, within the bound.
No kernel may reach another device: no remote copies, remote signals or barrier semaphores. Data moves between devices by JAX's collectives and lax.ppermute only.
A program may use at most 128 MiB of HBM per device.

```python
import math
import jax
import jax.numpy as jnp
import numpy as np
from jax import lax

D = 4096
EXPERTS = 128
TOPK = 8
FF = 1024
SPLIT = 4
TOK_DEV = 128
SECTIONS = 2
TOKENS = 2048
CAP = 12
N_EXPERT = 16


def block_scale(key, dims, cuts, least, high):
    loudness, own = 1.0, jax.random.fold_in(key, 6)
    for dim, shards_of in cuts:
        steps = jnp.exp(jax.random.uniform(jax.random.fold_in(own, dim), (shards_of,), jnp.float32, least / len(cuts), high / len(cuts)))
        loudness = loudness * jnp.repeat(steps, dims[dim] // shards_of).reshape([-1 if axis == dim else 1 for axis in range(len(dims))])
    return loudness


def assign_block(stream_key, own, number, rows, number_of, top, most, slope):
    ranking = jax.random.permutation(stream_key, number_of)
    heavy_load, ordinary = load_shares(number_of, rows * top, most, slope, True), load_shares(number_of, rows * top, most, slope, False)
    places = jnp.arange(number_of)

    def named(sizes, offset_by):
        used = int((sizes > 0).sum())
        fixed = max(1, used // 4)
        passed = fixed + (places - fixed + offset_by * (used - fixed)) % max(1, number_of - fixed)
        return jnp.zeros((number_of,), jnp.int32).at[ranking[jnp.where(places < fixed, places, passed)]].set(jnp.asarray(sizes, jnp.int32))

    sizes = jnp.where(number % 4 == 0, named(heavy_load, number // 4), named(ordinary, number - number // 4 - 1))
    mixed = jax.random.permutation(jax.random.fold_in(own, 3), number_of)
    donor, taker = mixed[0:number_of // 2 * 2:2], mixed[1:number_of // 2 * 2:2]
    margin = jnp.minimum(sizes[donor] - 1, most - sizes[taker]) // 2
    margin = jnp.where((donor == ranking[0]) | (taker == ranking[0]) | (sizes[taker] == 0), 0, jnp.maximum(margin, 0))
    passed = jax.random.randint(jax.random.fold_in(own, 4), (number_of // 2,), 0, 1 << 20) % (margin + 1)
    sizes = sizes.at[donor].add(-passed).at[taker].add(passed)
    members = jnp.searchsorted(jnp.cumsum(sizes), jnp.arange(rows * top), side="right").astype(jnp.int32)
    table = members.reshape(top, rows).T
    table = table[jax.random.permutation(jax.random.fold_in(own, 1), rows)]
    offset_by = jax.random.randint(jax.random.fold_in(own, 2), (rows, 1), 0, top)
    return jnp.take_along_axis(table, (jnp.arange(top)[None, :] + offset_by) % top, axis=1)


def load_shares(count, total, bound, slope, full):
    loads = [(1 << 20) // math.isqrt(rank ** slope) + 1 for rank in range(1, count + 1)]
    largest = bound if full else min(bound, max(-(-total // count), total * loads[0] // sum(loads)))
    least = 1 if total - largest >= count - 1 else 0
    holding, rest = [largest] + [least] * (count - 1), total - largest - least * (count - 1)
    while rest > 0:
        candidates = [i for i in range(1, count) if holding[i] < largest] or [i for i in range(1, count) if holding[i] < bound]
        mass, remaining = sum([loads[i] for i in candidates]), rest
        for i in candidates:
            extra = min(bound - holding[i], max(1, remaining * loads[i] // mass), rest)
            holding[i] = holding[i] + extra
            rest = rest - extra
    return np.array(holding)


def noise(rng, shape, deviation, bound, cuts=(), kind=jnp.bfloat16):
    loudness = block_scale(rng, shape, cuts, -0.22, 0.18) if cuts else 1.0
    values = jax.random.normal(rng, shape, jnp.float32) * deviation * loudness
    return jnp.minimum(jnp.maximum(values, -bound), bound).astype(kind)


def setup_inputs(seed: int = 0) -> dict:
    splits = jax.random.split(jax.random.key(seed), 12)
    x_first = noise(splits[0], (SECTIONS, TOKENS, D), 1.0, 6.0, ((0, 2), (1, 16)))
    grad_first = noise(splits[1], (SECTIONS, TOKENS, D), 2.0, 12.0, ((0, 2), (1, 16)))
    x_second = noise(splits[2], (SECTIONS, TOKENS, D), 1.0, 6.0, ((0, 2), (1, 16)))
    grad_last = noise(splits[3], (TOKENS, D), 2.0, 12.0, ((0, 16),))
    ids_first_keys = jax.random.split(jax.random.fold_in(splits[4], 1), SECTIONS * TOKENS // TOK_DEV)
    ids_first_turns = jax.random.permutation(jax.random.fold_in(splits[4], 3), SECTIONS * TOKENS // TOK_DEV)
    ids_first = jax.vmap(lambda own, number: assign_block(jax.random.fold_in(splits[4], 2), own, number, TOK_DEV, EXPERTS, TOPK, CAP, 2))(ids_first_keys, ids_first_turns).reshape((SECTIONS, TOKENS, TOPK))
    probs_first = jnp.clip(jnp.exp(math.log(1.0) - 2.9957323 * jax.random.uniform(splits[5], (SECTIONS, TOKENS, TOPK), jnp.float32) ** block_scale(splits[5], (SECTIONS, TOKENS, TOPK), ((0, 2), (1, 16)), -0.2, 0.2)), 0.05, 1.0)
    ids_second_keys = jax.random.split(jax.random.fold_in(splits[6], 1), SECTIONS * TOKENS // TOK_DEV)
    ids_second_turns = jax.random.permutation(jax.random.fold_in(splits[6], 3), SECTIONS * TOKENS // TOK_DEV)
    ids_second = jax.vmap(lambda own, number: assign_block(jax.random.fold_in(splits[6], 2), own, number, TOK_DEV, EXPERTS, TOPK, CAP, 2))(ids_second_keys, ids_second_turns).reshape((SECTIONS, TOKENS, TOPK))
    probs_second = jnp.clip(jnp.exp(math.log(1.0) - 2.9957323 * jax.random.uniform(splits[7], (SECTIONS, TOKENS, TOPK), jnp.float32) ** block_scale(splits[7], (SECTIONS, TOKENS, TOPK), ((0, 2), (1, 16)), -0.2, 0.2)), 0.05, 1.0)
    w_gate = noise(splits[8], (SECTIONS, N_EXPERT, D, FF // SPLIT), D ** -0.5, 0.09375, ((0, 2), (1, 16)))
    w_up = noise(splits[9], (SECTIONS, N_EXPERT, D, FF // SPLIT), D ** -0.5, 0.09375, ((0, 2), (1, 16)))
    w_down = noise(splits[10], (SECTIONS, N_EXPERT, FF // SPLIT, D), FF ** -0.5, 0.1875, ((0, 2), (1, 16)))
    return dict(x_first=x_first, grad_first=grad_first, x_second=x_second, grad_last=grad_last, ids_first=ids_first, probs_first=probs_first, ids_second=ids_second, probs_second=probs_second, w_gate=w_gate, w_up=w_up, w_down=w_down)


def expert_back(inputs, row_grads, gate_w, up_w, down_w):
    gate_pre = jnp.dot(inputs, gate_w, preferred_element_type=jnp.float32)
    up_pre = jnp.dot(inputs, up_w, preferred_element_type=jnp.float32)
    grad_act = jnp.dot(row_grads, down_w.T, preferred_element_type=jnp.float32)
    sigmoid_gate = jax.nn.sigmoid(gate_pre)
    grad_up = (grad_act * gate_pre * sigmoid_gate).astype(jnp.bfloat16)
    grad_gate = (grad_act * up_pre * sigmoid_gate * (1.0 + gate_pre * (1.0 - sigmoid_gate))).astype(jnp.bfloat16)
    return (jnp.dot(grad_gate, gate_w.T, preferred_element_type=jnp.float32)
            + jnp.dot(grad_up, up_w.T, preferred_element_type=jnp.float32))


def layer_back(inputs, grads, expert_ids, probs, w_gate, w_up, w_down):
    window = w_gate.shape[0] // SPLIT
    width = w_gate.shape[1]
    part_width = w_gate.shape[2]
    gate_full = w_gate.reshape(window, SPLIT, width, part_width).transpose(0, 2, 1, 3).reshape(window, width, SPLIT * part_width)
    up_full = w_up.reshape(window, SPLIT, width, part_width).transpose(0, 2, 1, 3).reshape(window, width, SPLIT * part_width)
    down_full = w_down.reshape(window, SPLIT * part_width, width)
    weights = probs / jnp.sum(probs, axis=-1, keepdims=True)
    slot_total = N_EXPERT * CAP

    def one_expert(running, operands):
        expert, gate_w, up_w, down_w = operands
        coef_row = jnp.sum(jnp.where(expert_ids == expert, weights, 0.0), axis=-1)
        chosen = jnp.any(expert_ids == expert, axis=-1)
        picked = jnp.nonzero(chosen, size=slot_total, fill_value=0)[0].astype(jnp.int32)
        count = jnp.sum(chosen.astype(jnp.int32))
        valid = jnp.arange(slot_total, dtype=jnp.int32) < count
        coef_rows = jnp.where(valid, coef_row[picked], 0.0)
        row_grads = (coef_rows[:, None] * grads[picked].astype(jnp.float32)).astype(jnp.bfloat16)
        contrib = expert_back(inputs[picked], row_grads, gate_w, up_w, down_w)
        contrib = jnp.where(valid[:, None], contrib, 0.0)
        return running.at[picked].add(contrib), None

    running, unused = lax.scan(one_expert, jnp.zeros(grads.shape, jnp.float32),
                               (jnp.arange(window, dtype=jnp.int32), gate_full, up_full, down_full))
    return running.astype(jnp.bfloat16)


def run_layer(operands):
    return layer_back(*operands)


def reference(x_first, grad_first, x_second, grad_last, ids_first, probs_first, ids_second, probs_second, w_gate, w_up, w_down):
    first = lax.map(run_layer, (x_first, grad_first, ids_first, probs_first, w_gate, w_up, w_down))
    incoming = jnp.concatenate([first[1:], grad_last[None]], axis=0)
    second = lax.map(run_layer, (x_second, incoming, ids_second, probs_second, w_gate, w_up, w_down))
    return first, second
```

```python
import functools

import jax
import jax.numpy as jnp
from jax import lax
from jax.experimental import pallas as pl
from jax.experimental.pallas import tpu as pltpu
from jax.sharding import PartitionSpec as P

EXPERTS = 128
SPLIT = 4
F32, BF16 = jnp.float32, jnp.bfloat16
VMEM_BYTES = 48 * 1024 * 1024


def call(body, outs, args, flops=0, bytes_moved=0):
    return pl.pallas_call(
        body,
        out_shape=outs,
        in_specs=[pl.BlockSpec(memory_space=pltpu.VMEM)] * len(args),
        out_specs=jax.tree.map(lambda _: pl.BlockSpec(memory_space=pltpu.VMEM), outs),
        compiler_params=pltpu.CompilerParams(vmem_limit_bytes=VMEM_BYTES),
        cost_estimate=pl.CostEstimate(
            flops=flops, bytes_accessed=bytes_moved, transcendentals=0
        ),
    )(*args)


def tables(ids, window, cap, probs=None):
    me = lax.axis_index("expert") // SPLIT
    tok = ids.shape[0]
    ids_t = jnp.transpose(ids)
    weights = None
    if probs is not None:
        probs_t = jnp.transpose(probs)
        weights = probs_t / jnp.sum(probs_t, axis=0, keepdims=True)
    named, coefs = [], []
    for k in range(window):
        match = ids_t == (me ^ k)
        named.append(jnp.sum(jnp.where(match, 1.0, 0.0), axis=0, keepdims=True))
        if probs is not None:
            coefs.append(jnp.sum(jnp.where(match, weights, 0.0), axis=0, keepdims=True))
    pad = [jnp.zeros((-window % 8, tok), F32)] if window % 8 else []
    stacked = jnp.concatenate(named + pad, axis=0).astype(BF16)
    before = (
        lax.broadcasted_iota(jnp.int32, (tok, tok), 0)
        < lax.broadcasted_iota(jnp.int32, (tok, tok), 1)
    ).astype(F32).astype(BF16)
    place = jnp.dot(stacked, before, preferred_element_type=F32)
    rows = lax.broadcasted_iota(jnp.int32, (2 * cap, tok), 0).astype(F32)
    top, bot, coef = [], [], []
    for k in range(window):
        slot = jnp.where(named[k] > 0.0, place[k : k + 1], -1000.0)
        upper = jnp.where(rows == slot, 1.0, 0.0)
        lower = jnp.where(rows == slot + cap, 1.0, 0.0)
        top.append(upper)
        bot.append(lower)
        if probs is not None:
            coef.append(jnp.sum((upper + lower) * coefs[k], axis=1, keepdims=True))
    top, bot = jnp.concatenate(top, axis=0), jnp.concatenate(bot, axis=0)
    return top, bot, jnp.concatenate(coef, axis=0) if coef else None


def gathered(top, bot, rows):
    half = rows.shape[1] // 2
    return jnp.dot(top.astype(BF16), rows[:, :half], preferred_element_type=F32) + jnp.dot(
        bot.astype(BF16), rows[:, half:], preferred_element_type=F32
    )


def pack_pair(window, cap, ids_ref, probs_ref, x_ref, grad_ref, *out_refs):
    top, bot, coef = tables(ids_ref[0], window, cap, probs_ref[0])
    picked_x = gathered(top, bot, x_ref[0])
    picked_grad = gathered(top, bot, grad_ref[0]) * coef
    for k in range(window):
        part = slice(2 * cap * k, 2 * cap * (k + 1))
        out_refs[k][0] = picked_x[part].astype(BF16)
        out_refs[k][1] = picked_grad[part].astype(BF16)


def pack_x(window, cap, ids_ref, x_ref, *out_refs):
    top, bot, _ = tables(ids_ref[0], window, cap)
    picked_x = gathered(top, bot, x_ref[0])
    for k in range(window):
        out_refs[k][...] = picked_x[2 * cap * k : 2 * cap * (k + 1)].astype(BF16)


def scattered(ids_ref, window, cap, blocks):
    top, bot, _ = tables(ids_ref[0], window, cap)
    rows = jnp.concatenate([b[...].astype(F32) for b in blocks], axis=0).astype(BF16)
    turned = (((0,), (0,)), ((), ()))
    left = lax.dot_general(top.astype(BF16), rows, turned, preferred_element_type=F32)
    right = lax.dot_general(bot.astype(BF16), rows, turned, preferred_element_type=F32)
    return left.astype(BF16), right.astype(BF16)


def relay(window, cap, ids_ref, ids_next_ref, probs_next_ref, grad_last_ref, *refs):
    blocks, dx_ref, out_refs = refs[:window], refs[window], refs[window + 1 :]
    left, right = scattered(ids_ref, window, cap, blocks)
    half = left.shape[1]
    dx_ref[0, :, :half] = left
    dx_ref[0, :, half:] = right
    opening = lax.axis_index("pipe") == 0
    left = jnp.where(opening, grad_last_ref[:, :half], left)
    right = jnp.where(opening, grad_last_ref[:, half:], right)
    top, bot, coef = tables(ids_next_ref[0], window, cap, probs_next_ref[0])
    picked = coef * (
        jnp.dot(top.astype(BF16), left, preferred_element_type=F32)
        + jnp.dot(bot.astype(BF16), right, preferred_element_type=F32)
    )
    for k in range(window):
        out_refs[k][...] = picked[2 * cap * k : 2 * cap * (k + 1)].astype(BF16)


def finish(window, cap, ids_ref, *refs):
    blocks, dx_ref = refs[:window], refs[window]
    left, right = scattered(ids_ref, window, cap, blocks)
    half = left.shape[1]
    dx_ref[0, :, :half] = left
    dx_ref[0, :, half:] = right


NT = (((1,), (1,)), ((), ()))


def joined(blocks):
    return jnp.concatenate([b.astype(F32) for b in blocks], axis=0).astype(BF16)


def factors(rows, cap, gate_ref, up_ref):
    half = rows.shape[1]

    def product(ref):
        lower = jnp.dot(rows, ref[half:, :], preferred_element_type=F32)
        return jnp.dot(rows, ref[:half, :], preferred_element_type=F32) + pltpu.roll(
            lower, rows.shape[0] - cap, 0
        )

    gate, up = product(gate_ref), product(up_ref)
    sig = jax.nn.sigmoid(gate)
    return gate * sig, up * sig * (1.0 + gate * (1.0 - sig))


def input_grads(rows, cap, halves, scales, own_ref, far_ref):
    count, half = rows.shape
    valid = lax.broadcasted_iota(jnp.int32, (count, 1), 0) % (2 * cap) < cap
    lhs = []
    for (gate_ref, up_ref, down_ref), (for_up, for_gate) in zip(halves, scales):
        lower = lax.dot_general(rows, down_ref[:, half:], NT, preferred_element_type=F32)
        back = lax.dot_general(
            rows, down_ref[:, :half], NT, preferred_element_type=F32
        ) + pltpu.roll(lower, count - cap, 0)
        d_up = jnp.where(valid, back * for_up, 0.0)
        d_gate = jnp.where(valid, back * for_gate, 0.0)
        lhs.append(
            (
                (d_gate.astype(BF16), pltpu.roll(d_gate, cap, 0).astype(BF16), gate_ref),
                (d_up.astype(BF16), pltpu.roll(d_up, cap, 0).astype(BF16), up_ref),
            )
        )
    step = 256
    own_rows = own_ref.shape[0]
    for n in range(0, half, step):
        total = None
        for pair in lhs:
            for upper, lower, ref in pair:
                term = lax.dot_general(
                    upper, ref[n : n + step, :], NT, preferred_element_type=F32
                ) + lax.dot_general(
                    lower, ref[half + n : half + n + step, :], NT, preferred_element_type=F32
                )
                total = term if total is None else total + term
        own_ref[:, n : n + step] = total[:own_rows]
        far_ref[:, n : n + step] = total[own_rows:].astype(BF16)


def whole_unit(blocks, cap, *refs):
    ins, weights, (own_ref, far_ref) = refs[:blocks], refs[blocks:-2], refs[-2:]
    x_rows = joined([b[0] for b in ins])
    grad_rows = joined([b[1] for b in ins])
    halves = (weights[:3], weights[3:])
    scales = [factors(x_rows, cap, g, u) for g, u, _ in halves]
    input_grads(grad_rows, cap, halves, scales, own_ref, far_ref)


def unit_x(blocks, cap, *refs):
    ins, weights, out_ref = refs[:blocks], refs[blocks:-1], refs[-1]
    x_rows = joined([b[...] for b in ins])
    for i in range(2):
        out_ref[2 * i], out_ref[2 * i + 1] = factors(x_rows, cap, *weights[2 * i : 2 * i + 2])


def unit_grad(blocks, cap, *refs):
    ins, scale_ref, weights, (own_ref, far_ref) = (
        refs[:blocks],
        refs[blocks],
        refs[blocks + 1 : -2],
        refs[-2:],
    )
    grad_rows = joined([b[...] for b in ins])
    scales = [(scale_ref[2 * i], scale_ref[2 * i + 1]) for i in range(2)]
    input_grads(grad_rows, cap, (weights[:3], weights[3:]), scales, own_ref, far_ref)


def add_far(window, cap, own_ref, far_ref, *out_refs):
    for k in range(window):
        part = slice(2 * cap * k, 2 * cap * (k + 1))
        out_refs[k][...] = (own_ref[part] + far_ref[part].astype(F32)).astype(BF16)


def body(
    x_first,
    grad_first,
    x_second,
    grad_last,
    ids_first,
    probs_first,
    ids_second,
    probs_second,
    w_gate,
    w_up,
    w_down,
):
    tok, width = x_first.shape[1:]
    topk = ids_first.shape[2]
    devices = lax.axis_size("expert")
    sections = lax.axis_size("pipe")
    window = devices // SPLIT
    cap = 3 * tok * topk // (2 * EXPERTS)
    half = width // 2
    shape = jax.ShapeDtypeStruct

    def send(x, bits):
        return lax.ppermute(x, "expert", [(i, i ^ bits) for i in range(devices)])

    def plane(x, k):
        return send(x, SPLIT * k) if k else x

    def across(x):
        return send(x, 2)

    order = list(range(window))[::-1]
    own_w = (w_gate[0, 0], w_up[0, 0], w_down[0, 0])
    msg = shape((2 * cap, half), BF16)
    pair = shape((2, 2 * cap, half), BF16)
    weights = own_w + tuple(send(w, 1) for w in own_w)
    ring = [(s, (s + 1) % sections) for s in range(sections)]
    ids_next, probs_next = (
        lax.ppermute(a, "pipe", ring) for a in (ids_second, probs_second)
    )

    def spread(msgs):
        near = [None] * window
        far = [None] * window
        for k in order:
            near[k] = plane(msgs[k], k)
        for k in order[::-1]:
            far[k] = across(near[k])
        return near + far

    def bring_back(own, far):
        far = across(far)
        sums = call(
            functools.partial(add_far, window, cap),
            [msg] * window,
            (own, far),
        )
        back = [None] * window
        for k in order:
            back[k] = plane(sums[k], k)
        return back

    rows = window * 2 * cap
    partial_shapes = [shape((rows, half), F32), shape((rows, half), BF16)]

    first = call(
        functools.partial(pack_pair, window, cap),
        [pair] * window,
        (ids_first, probs_first, x_first, grad_first),
    )
    first = spread(first)
    second_x = call(
        functools.partial(pack_x, window, cap), [msg] * window, (ids_second, x_second)
    )
    own, far = call(
        functools.partial(whole_unit, 2 * window, cap), partial_shapes, (*first, *weights)
    )
    back = bring_back(own, far)
    second_x = spread(second_x)
    scales = call(
        functools.partial(unit_x, 2 * window, cap),
        shape((4, 2 * rows, w_gate.shape[3]), F32),
        (*second_x, weights[0], weights[1], weights[3], weights[4]),
    )
    dx_first, *grads = call(
        functools.partial(relay, window, cap),
        [shape((1, tok, width), BF16)] + [msg] * window,
        (ids_first, ids_next, probs_next, grad_last, *back),
    )
    near = [None] * window
    for k in order:
        pairs = [
            (s * devices + i, (s - 1) % sections * devices + (i ^ (SPLIT * k)))
            for s in range(sections)
            for i in range(devices)
        ]
        near[k] = lax.ppermute(grads[k], ("pipe", "expert"), pairs)
    grads = near + [across(near[k]) for k in range(window)]
    own, far = call(
        functools.partial(unit_grad, 2 * window, cap), partial_shapes, (*grads, scales, *weights)
    )
    back = bring_back(own, far)
    dx_second = call(
        functools.partial(finish, window, cap),
        shape((1, tok, width), BF16),
        (ids_second, *back),
    )
    return dx_first, dx_second


def solution(mesh):
    split = P("pipe", "expert", None)
    stacked = P("pipe", "expert", None, None)
    return jax.shard_map(
        body,
        mesh=mesh,
        in_specs=(
            split,
            split,
            split,
            P("expert", None),
            split,
            split,
            split,
            split,
            stacked,
            stacked,
            stacked,
        ),
        out_specs=(split, split),
        check_vma=False,
    )
```

```python
import functools

import jax
import jax.numpy as jnp
from jax import lax
from jax.experimental import pallas as pl
from jax.experimental.pallas import tpu as pltpu
from jax.sharding import PartitionSpec as P

EXPERTS = 128
SPLIT = 4
F32, BF16 = jnp.float32, jnp.bfloat16
MIB = 1024 * 1024
COMPUTE_MIB = 26
PACK_MIB = 44


def call(body, outs, args, mib, away=(), scratch=(), us=1.0):
    return pl.pallas_call(
        body,
        out_shape=outs,
        in_specs=[
            pl.BlockSpec(memory_space=pl.ANY if i in away else pltpu.VMEM)
            for i in range(len(args))
        ],
        out_specs=jax.tree.map(lambda _: pl.BlockSpec(memory_space=pltpu.VMEM), outs),
        scratch_shapes=scratch,
        compiler_params=pltpu.CompilerParams(vmem_limit_bytes=mib * MIB),
        cost_estimate=pl.CostEstimate(
            flops=0, bytes_accessed=int(us * 3.6e6), transcendentals=0
        ),
    )(*args)


def fetch(pairs, sems):
    copies = [pltpu.make_async_copy(a, b, sems.at[i]) for i, (a, b) in enumerate(pairs)]
    for c in copies:
        c.start()
    return copies


def row_parts(ref, buf, parts=4):
    step = buf.shape[0] // parts
    return [(ref.at[pl.ds(step * i, step)], buf.at[pl.ds(step * i, step)]) for i in range(parts)]


def sequence(window):
    return [k for k in range(2, window)] + [1, 0][-window:]


def tables(ids_t, window, cap, probs_t=None):
    me = lax.axis_index("expert") // SPLIT
    tok = ids_t.shape[1]
    weights = None
    if probs_t is not None:
        weights = probs_t / jnp.sum(probs_t, axis=0, keepdims=True)
    named, coefs = [], []
    for k in range(window):
        match = ids_t == (me ^ sequence(window)[k])
        named.append(jnp.sum(jnp.where(match, 1.0, 0.0), axis=0, keepdims=True))
        if probs_t is not None:
            coefs.append(jnp.sum(jnp.where(match, weights, 0.0), axis=0, keepdims=True))
    pad = [jnp.zeros((-window % 8, tok), F32)] if window % 8 else []
    stacked = jnp.concatenate(named + pad, axis=0).astype(BF16)
    before = (
        lax.broadcasted_iota(jnp.int32, (tok, tok), 0)
        < lax.broadcasted_iota(jnp.int32, (tok, tok), 1)
    ).astype(F32).astype(BF16)
    place = jnp.dot(stacked, before, preferred_element_type=F32)
    rows = lax.broadcasted_iota(jnp.int32, (2 * cap, tok), 0).astype(F32)
    top, bot, coef = [], [], []
    for k in range(window):
        slot = jnp.where(named[k] > 0.0, place[k : k + 1], -1000.0)
        upper = jnp.where(rows == slot, 1.0, 0.0)
        lower = jnp.where(rows == slot + cap, 1.0, 0.0)
        top.append(upper)
        bot.append(lower)
        if probs_t is not None:
            coef.append(jnp.sum((upper + lower) * coefs[k], axis=1, keepdims=True))
    top, bot = jnp.concatenate(top, axis=0), jnp.concatenate(bot, axis=0)
    return top, bot, jnp.concatenate(coef, axis=0) if coef else None


def gathered(top, bot, rows):
    half = rows.shape[1] // 2
    return jnp.dot(top.astype(BF16), rows[:, :half], preferred_element_type=F32) + jnp.dot(
        bot.astype(BF16), rows[:, half:], preferred_element_type=F32
    )


def pack_x(window, cap, ids_ref, x_ref, *refs):
    out_refs, (x_buf, sems) = refs[-2 - window : -2], refs[-2:]
    copies = fetch(row_parts(x_ref, x_buf), sems)
    top, bot, _ = tables(ids_ref[...], window, cap)
    for c in copies:
        c.wait()
    picked = gathered(top, bot, x_buf[...])
    for k in range(window):
        out_refs[k][...] = picked[2 * cap * k : 2 * cap * (k + 1)].astype(BF16)


def pack_grad(window, cap, ids_ref, probs_ref, ids_on_ref, probs_on_ref, grad_ref, *refs):
    keys_ref, *out_refs = refs[-3 - window : -2]
    grad_buf, sems = refs[-2:]
    topk = ids_on_ref.shape[0]
    keys_ref[:topk] = ids_on_ref[...].astype(F32)
    keys_ref[topk:] = probs_on_ref[...]
    copies = fetch(row_parts(grad_ref, grad_buf), sems)
    top, bot, coef = tables(ids_ref[...], window, cap, probs_ref[...])
    for c in copies:
        c.wait()
    picked = gathered(top, bot, grad_buf[...]) * coef
    for k in range(window):
        out_refs[k][...] = picked[2 * cap * k : 2 * cap * (k + 1)].astype(BF16)


def scattered(ids_ref, window, cap, blocks):
    top, bot, _ = tables(ids_ref[...], window, cap)
    rows = jnp.concatenate([b[...].astype(F32) for b in blocks], axis=0).astype(BF16)
    turned = (((0,), (0,)), ((), ()))
    left = lax.dot_general(top.astype(BF16), rows, turned, preferred_element_type=F32)
    right = lax.dot_general(bot.astype(BF16), rows, turned, preferred_element_type=F32)
    return left.astype(BF16), right.astype(BF16)


def relay(window, cap, ids_ref, keys_ref, grad_last_ref, *refs):
    topk = ids_ref.shape[0]
    blocks, dx_ref, out_refs = refs[:window], refs[window], refs[window + 1 : -2]
    grad_buf, sems = refs[-2:]
    copies = fetch(row_parts(grad_last_ref, grad_buf), sems)
    left, right = scattered(ids_ref, window, cap, blocks)
    half = left.shape[1]
    dx_ref[0, :, :half] = left
    dx_ref[0, :, half:] = right
    top, bot, coef = tables(
        keys_ref[:topk].astype(jnp.int32), window, cap, keys_ref[topk:]
    )
    for c in copies:
        c.wait()
    opening = lax.axis_index("pipe") == 0
    left = jnp.where(opening, grad_buf[:, :half], left)
    right = jnp.where(opening, grad_buf[:, half:], right)
    picked = coef * (
        jnp.dot(top.astype(BF16), left, preferred_element_type=F32)
        + jnp.dot(bot.astype(BF16), right, preferred_element_type=F32)
    )
    for k in range(window):
        out_refs[k][...] = picked[2 * cap * k : 2 * cap * (k + 1)].astype(BF16)


def finish(window, cap, ids_ref, *refs):
    blocks, dx_ref = refs[:window], refs[window]
    left, right = scattered(ids_ref, window, cap, blocks)
    half = left.shape[1]
    dx_ref[0, :, :half] = left
    dx_ref[0, :, half:] = right


NT = (((1,), (1,)), ((), ()))


def joined(blocks):
    return jnp.concatenate([b.astype(F32) for b in blocks], axis=0).astype(BF16)


def factors(rows, cap, gate_ref, up_ref):
    half = rows.shape[1]

    def product(ref):
        lower = jnp.dot(rows, ref[half:, :], preferred_element_type=F32)
        return jnp.dot(rows, ref[:half, :], preferred_element_type=F32) + pltpu.roll(
            lower, rows.shape[0] - cap, 0
        )

    gate, up = product(gate_ref), product(up_ref)
    sig = jax.nn.sigmoid(gate)
    return gate * sig, up * sig * (1.0 + gate * (1.0 - sig))


def hidden_grads(rows, cap, down_ref, for_up, for_gate):
    count, half = rows.shape
    valid = lax.broadcasted_iota(jnp.int32, (count, 1), 0) % (2 * cap) < cap
    lower = lax.dot_general(rows, down_ref[:, half:], NT, preferred_element_type=F32)
    back = lax.dot_general(
        rows, down_ref[:, :half], NT, preferred_element_type=F32
    ) + pltpu.roll(lower, count - cap, 0)
    d_up = jnp.where(valid, back * for_up, 0.0)
    d_gate = jnp.where(valid, back * for_gate, 0.0)
    return [
        (d.astype(BF16), pltpu.roll(d, cap, 0).astype(BF16)) for d in (d_gate, d_up)
    ]


def input_grads(lhs, refs, own_refs, far_refs, step=256):
    half = own_refs[0].shape[1]
    for n in range(0, half, step):
        total = None
        for (upper, lower), ref in zip(lhs, refs):
            term = lax.dot_general(
                upper, ref[n : n + step, :], NT, preferred_element_type=F32
            ) + lax.dot_general(
                lower, ref[half + n : half + n + step, :], NT, preferred_element_type=F32
            )
            total = term if total is None else total + term
        row = 0
        for ref in (*own_refs, *far_refs):
            ref[:, n : n + step] = total[row : row + ref.shape[0]].astype(ref.dtype)
            row += ref.shape[0]


def unit_x(blocks, cap, *refs):
    ins, weights, out_ref, bufs, sems = (
        refs[:blocks],
        refs[blocks : blocks + 4],
        refs[blocks + 4],
        refs[blocks + 5 : -1],
        refs[-1],
    )
    copies = fetch(list(zip(weights, bufs)), sems)
    x_rows = joined([b[...] for b in ins])
    for i in range(2):
        copies[2 * i].wait()
        copies[2 * i + 1].wait()
        out_ref[2 * i], out_ref[2 * i + 1] = factors(x_rows, cap, bufs[2 * i], bufs[2 * i + 1])


def unit_grad(blocks, cap, *refs):
    ins, scale_ref = refs[:blocks], refs[blocks]
    weights, outs = refs[blocks + 1 : blocks + 7], refs[blocks + 7 : -7]
    bufs, sems = refs[-7:-1], refs[-1]
    copies = fetch([(weights[i], bufs[i]) for i in (2, 5, 0, 1, 3, 4)], sems)
    grad_rows = joined([b[...] for b in ins])
    lhs = []
    for i in range(2):
        copies[i].wait()
        lhs += hidden_grads(grad_rows, cap, bufs[3 * i + 2], scale_ref[2 * i], scale_ref[2 * i + 1])
    for c in copies[2:]:
        c.wait()
    groups = len(outs) // 2
    input_grads(lhs, [bufs[i] for i in (0, 1, 3, 4)], outs[:groups], outs[groups:])


def add_far(cap, own_ref, far_ref, *out_refs):
    for k, out_ref in enumerate(out_refs):
        part = slice(2 * cap * k, 2 * cap * (k + 1))
        out_ref[...] = (own_ref[part] + far_ref[part].astype(F32)).astype(BF16)


def body(
    x_first,
    grad_first,
    x_second,
    grad_last,
    ids_first,
    probs_first,
    ids_second,
    probs_second,
    w_gate,
    w_up,
    w_down,
):
    tok, width = x_first.shape[1:]
    topk = ids_first.shape[2]
    devices = lax.axis_size("expert")
    sections = lax.axis_size("pipe")
    window = devices // SPLIT
    cap = 3 * tok * topk // (2 * EXPERTS)
    half = width // 2
    shape = jax.ShapeDtypeStruct

    def send(x, bits):
        return lax.ppermute(x, "expert", [(i, i ^ bits) for i in range(devices)])

    def plane(x, k):
        return send(x, SPLIT * k) if k else x

    def across(x):
        return send(x, 2)

    own_w = (w_gate[0, 0], w_up[0, 0], w_down[0, 0])
    msg = shape((2 * cap, half), BF16)
    pair = shape((2, 2 * cap, half), BF16)
    weights = own_w + tuple(send(w, 1) for w in own_w)
    bufs = [pltpu.VMEM(w.shape, BF16) for w in weights]
    dma = pltpu.SemaphoreType.DMA
    row_buf = pltpu.VMEM((tok, width), BF16)
    order = sequence(window)
    rows = window * 2 * cap
    after = lax.optimization_barrier

    ids_1, probs_1, ids_2, probs_2 = (
        jnp.swapaxes(a[0], 0, 1) for a in (ids_first, probs_first, ids_second, probs_second)
    )
    ring = [(s, (s + 1) % sections) for s in range(sections)]

    def listed(by_k):
        return [by_k[k] for k in order]

    def pack(ids, x, extra=()):
        made = call(
            functools.partial(pack_x, window, cap),
            [msg] * window,
            (ids, x, *extra),
            PACK_MIB if not extra else 16,
            away=range(1, 2 + len(extra)),
            scratch=[row_buf, dma((4,))],
            us=3.0,
        )
        return dict(zip(order, made))

    def forward(near, far):
        return call(
            functools.partial(unit_x, 2 * window, cap),
            shape((4, 2 * rows, w_gate.shape[3]), F32),
            (*listed(near), *listed(far), weights[0], weights[1], weights[3], weights[4]),
            COMPUTE_MIB,
            away=range(2 * window, 2 * window + 4),
            scratch=[bufs[0], bufs[1], bufs[3], bufs[4], dma((4,))],
            us=2.7,
        )

    groups = [order[:-2], order[-2:]] if window > 2 else [order]
    heights = [2 * cap * len(g) for g in groups]

    def backward(near, far, scales):
        made = call(
            functools.partial(unit_grad, 2 * window, cap),
            [shape((h, half), F32) for h in heights] + [shape((h, half), BF16) for h in heights],
            (*listed(near), *listed(far), scales, *weights),
            COMPUTE_MIB,
            away=range(2 * window + 1, 2 * window + 7),
            scratch=[*bufs, dma((6,))],
            us=5.7,
        )
        back = {}
        for group, own, far in zip(groups, made, made[len(groups) :]):
            far = across(far)
            sums = call(functools.partial(add_far, cap), [msg] * len(group), (own, far), 8)
            back.update({k: plane(sums[j], k) for j, k in enumerate(group)})
        return far, listed(back)

    x_1 = pack(ids_1, x_first[0])
    keys, *grad_1 = call(
        functools.partial(pack_grad, window, cap),
        [shape((2 * topk, tok), F32)] + [msg] * window,
        (ids_1, probs_1, ids_2, probs_2, grad_first[0], x_1[0]),
        PACK_MIB,
        away=(4, 5),
        scratch=[row_buf, dma((4,))],
        us=3.0,
    )
    grad_1 = dict(zip(order, grad_1))
    outer = [k for k in order if k > 1]
    near_x = {k: plane(x_1[k], k) for k in outer}
    near_x, grad_1, *peer_w = after((near_x, grad_1, *weights[3:]))
    weights = own_w + tuple(peer_w)
    near_g = {k: plane(grad_1[k], k) for k in outer}
    for k in (1, 0):
        near_x[k] = plane(x_1[k], k)
        near_g[k] = plane(grad_1[k], k)
    far_x = {k: across(near_x[k]) for k in (0, 1, *outer)}
    far_g = {k: across(near_g[k]) for k in (0, 1, *outer)}
    keys = lax.ppermute(after((keys, near_x[1]))[0], "pipe", ring)
    x_2 = pack(ids_2, x_second[0], (near_g[outer[-1]], keys))
    near_x2 = {k: plane(x_2[k], k) for k in order}
    arrived, back = backward(near_g, far_g, forward(near_x, far_x))
    near_x2 = after((near_x2, arrived))[0]
    far_x2 = {k: across(near_x2[k]) for k in order}
    scales = forward(near_x2, far_x2)
    dx_first, *grads = call(
        functools.partial(relay, window, cap),
        [shape((1, tok, width), BF16)] + [msg] * window,
        (ids_1, keys, grad_last, *back),
        16,
        away=(2,),
        scratch=[row_buf, dma((4,))],
        us=1.8,
    )
    near = {}
    for j, k in enumerate(order):
        pairs = [
            (s * devices + i, (s - 1) % sections * devices + (i ^ (SPLIT * k)))
            for s in range(sections)
            for i in range(devices)
        ]
        near[k] = lax.ppermute(grads[j], ("pipe", "expert"), pairs)
    far = {k: across(near[k]) for k in order[::-1]}
    _, back = backward(near, far, scales)
    dx_second = call(
        functools.partial(finish, window, cap),
        shape((1, tok, width), BF16),
        (ids_2, *back),
        16,
    )
    return dx_first, dx_second


def solution(mesh):
    split = P("pipe", "expert", None)
    stacked = P("pipe", "expert", None, None)
    return jax.shard_map(
        body,
        mesh=mesh,
        in_specs=(
            split,
            split,
            split,
            P("expert", None),
            split,
            split,
            split,
            split,
            stacked,
            stacked,
            stacked,
        ),
        out_specs=(split, split),
        check_vma=False,
    )
```

```python
import functools

import jax
import jax.numpy as jnp
from jax import lax
from jax.experimental import pallas as pl
from jax.experimental.pallas import tpu as pltpu
from jax.sharding import PartitionSpec as P

EXPERTS = 128
SPLIT = 4
F32, BF16 = jnp.float32, jnp.bfloat16
MIB = 1024 * 1024
COMPUTE_MIB = 26
PACK_MIB = 44


def call(body, outs, args, mib, away=(), scratch=(), us=1.0):
    return pl.pallas_call(
        body,
        out_shape=outs,
        in_specs=[
            pl.BlockSpec(memory_space=pl.ANY if i in away else pltpu.VMEM)
            for i in range(len(args))
        ],
        out_specs=jax.tree.map(lambda _: pl.BlockSpec(memory_space=pltpu.VMEM), outs),
        scratch_shapes=scratch,
        compiler_params=pltpu.CompilerParams(vmem_limit_bytes=mib * MIB),
        cost_estimate=pl.CostEstimate(
            flops=0, bytes_accessed=int(us * 3.6e6), transcendentals=0
        ),
    )(*args)


def fetch(pairs, sems):
    copies = [pltpu.make_async_copy(a, b, sems.at[i]) for i, (a, b) in enumerate(pairs)]
    for c in copies:
        c.start()
    return copies


def row_parts(ref, buf, parts=4):
    step = buf.shape[0] // parts
    return [(ref.at[pl.ds(step * i, step)], buf.at[pl.ds(step * i, step)]) for i in range(parts)]


def sequence(window):
    return [k for k in range(2, window)] + [1, 0][-window:]


def tables(ids_t, window, cap, probs_t=None):
    me = lax.axis_index("expert") // SPLIT
    tok = ids_t.shape[1]
    weights = None
    if probs_t is not None:
        weights = probs_t / jnp.sum(probs_t, axis=0, keepdims=True)
    named, coefs = [], []
    for k in range(window):
        match = ids_t == (me ^ sequence(window)[k])
        named.append(jnp.sum(jnp.where(match, 1.0, 0.0), axis=0, keepdims=True))
        if probs_t is not None:
            coefs.append(jnp.sum(jnp.where(match, weights, 0.0), axis=0, keepdims=True))
    pad = [jnp.zeros((-window % 8, tok), F32)] if window % 8 else []
    stacked = jnp.concatenate(named + pad, axis=0).astype(BF16)
    before = (
        lax.broadcasted_iota(jnp.int32, (tok, tok), 0)
        < lax.broadcasted_iota(jnp.int32, (tok, tok), 1)
    ).astype(F32).astype(BF16)
    place = jnp.dot(stacked, before, preferred_element_type=F32)
    rows = lax.broadcasted_iota(jnp.int32, (2 * cap, tok), 0).astype(F32)
    top, bot, coef = [], [], []
    for k in range(window):
        slot = jnp.where(named[k] > 0.0, place[k : k + 1], -1000.0)
        upper = jnp.where(rows == slot, 1.0, 0.0)
        lower = jnp.where(rows == slot + cap, 1.0, 0.0)
        top.append(upper)
        bot.append(lower)
        if probs_t is not None:
            coef.append(jnp.sum((upper + lower) * coefs[k], axis=1, keepdims=True))
    top, bot = jnp.concatenate(top, axis=0), jnp.concatenate(bot, axis=0)
    return top, bot, jnp.concatenate(coef, axis=0) if coef else None


def gathered(top, bot, rows):
    half = rows.shape[1] // 2
    return jnp.dot(top.astype(BF16), rows[:, :half], preferred_element_type=F32) + jnp.dot(
        bot.astype(BF16), rows[:, half:], preferred_element_type=F32
    )


def pack_x(window, cap, ids_ref, x_ref, *refs):
    out_refs, (x_buf, sems) = refs[-2 - window : -2], refs[-2:]
    copies = fetch(row_parts(x_ref, x_buf), sems)
    top, bot, _ = tables(ids_ref[...], window, cap)
    for c in copies:
        c.wait()
    picked = gathered(top, bot, x_buf[...])
    for k in range(window):
        out_refs[k][...] = picked[2 * cap * k : 2 * cap * (k + 1)].astype(BF16)


def pack_rest(window, cap, ids_ref, probs_ref, ids_on_ref, probs_on_ref, grad_ref, x_ref, *refs):
    out_refs, (grad_buf, x_buf, sems) = refs[-4 - 2 * window : -3], refs[-3:]
    keys_ref, out_refs = out_refs[0], out_refs[1:]
    copies = fetch(row_parts(grad_ref, grad_buf) + row_parts(x_ref, x_buf), sems)
    topk = ids_on_ref.shape[0]
    keys_ref[:topk] = ids_on_ref[...].astype(F32)
    keys_ref[topk:] = probs_on_ref[...]
    top, bot, coef = tables(ids_ref[...], window, cap, probs_ref[...])
    top_on, bot_on, _ = tables(ids_on_ref[...], window, cap)
    for c in copies[:4]:
        c.wait()
    picked = gathered(top, bot, grad_buf[...]) * coef
    for k in range(window):
        out_refs[k][...] = picked[2 * cap * k : 2 * cap * (k + 1)].astype(BF16)
    for c in copies[4:]:
        c.wait()
    picked = gathered(top_on, bot_on, x_buf[...])
    for k in range(window):
        out_refs[window + k][...] = picked[2 * cap * k : 2 * cap * (k + 1)].astype(BF16)


def scattered(ids_ref, window, cap, blocks):
    top, bot, _ = tables(ids_ref[...], window, cap)
    rows = jnp.concatenate([b[...].astype(F32) for b in blocks], axis=0).astype(BF16)
    turned = (((0,), (0,)), ((), ()))
    left = lax.dot_general(top.astype(BF16), rows, turned, preferred_element_type=F32)
    right = lax.dot_general(bot.astype(BF16), rows, turned, preferred_element_type=F32)
    return left.astype(BF16), right.astype(BF16)


def relay(window, cap, ids_ref, keys_ref, grad_last_ref, *refs):
    topk = ids_ref.shape[0]
    blocks, dx_ref, out_refs = refs[:window], refs[window], refs[window + 1 : -2]
    grad_buf, sems = refs[-2:]
    copies = fetch(row_parts(grad_last_ref, grad_buf), sems)
    left, right = scattered(ids_ref, window, cap, blocks)
    half = left.shape[1]
    dx_ref[0, :, :half] = left
    dx_ref[0, :, half:] = right
    top, bot, coef = tables(
        keys_ref[:topk].astype(jnp.int32), window, cap, keys_ref[topk:]
    )
    for c in copies:
        c.wait()
    opening = lax.axis_index("pipe") == 0
    left = jnp.where(opening, grad_buf[:, :half], left)
    right = jnp.where(opening, grad_buf[:, half:], right)
    picked = coef * (
        jnp.dot(top.astype(BF16), left, preferred_element_type=F32)
        + jnp.dot(bot.astype(BF16), right, preferred_element_type=F32)
    )
    for k in range(window):
        out_refs[k][...] = picked[2 * cap * k : 2 * cap * (k + 1)].astype(BF16)


def finish(window, cap, ids_ref, *refs):
    blocks, dx_ref = refs[:window], refs[window]
    left, right = scattered(ids_ref, window, cap, blocks)
    half = left.shape[1]
    dx_ref[0, :, :half] = left
    dx_ref[0, :, half:] = right


NT = (((1,), (1,)), ((), ()))


def joined(blocks):
    return jnp.concatenate([b.astype(F32) for b in blocks], axis=0).astype(BF16)


def factors(rows, cap, gate_ref, up_ref):
    half = rows.shape[1]

    def product(ref):
        lower = jnp.dot(rows, ref[half:, :], preferred_element_type=F32)
        return jnp.dot(rows, ref[:half, :], preferred_element_type=F32) + pltpu.roll(
            lower, rows.shape[0] - cap, 0
        )

    gate, up = product(gate_ref), product(up_ref)
    sig = jax.nn.sigmoid(gate)
    return gate * sig, up * sig * (1.0 + gate * (1.0 - sig))


def hidden_grads(rows, cap, down_ref, for_up, for_gate):
    count, half = rows.shape
    valid = lax.broadcasted_iota(jnp.int32, (count, 1), 0) % (2 * cap) < cap
    lower = lax.dot_general(rows, down_ref[:, half:], NT, preferred_element_type=F32)
    back = lax.dot_general(
        rows, down_ref[:, :half], NT, preferred_element_type=F32
    ) + pltpu.roll(lower, count - cap, 0)
    d_up = jnp.where(valid, back * for_up, 0.0)
    d_gate = jnp.where(valid, back * for_gate, 0.0)
    return [
        (d.astype(BF16), pltpu.roll(d, cap, 0).astype(BF16)) for d in (d_gate, d_up)
    ]


def input_grads(lhs, refs, own_refs, far_refs, step=256):
    half = own_refs[0].shape[1]
    for n in range(0, half, step):
        total = None
        for (upper, lower), ref in zip(lhs, refs):
            term = lax.dot_general(
                upper, ref[n : n + step, :], NT, preferred_element_type=F32
            ) + lax.dot_general(
                lower, ref[half + n : half + n + step, :], NT, preferred_element_type=F32
            )
            total = term if total is None else total + term
        row = 0
        for ref in (*own_refs, *far_refs):
            ref[:, n : n + step] = total[row : row + ref.shape[0]].astype(ref.dtype)
            row += ref.shape[0]


def unit_x(blocks, cap, *refs):
    ins, weights, out_ref, bufs, sems = (
        refs[:blocks],
        refs[blocks : blocks + 4],
        refs[-6],
        refs[-5:-1],
        refs[-1],
    )
    copies = fetch(list(zip(weights, bufs)), sems)
    x_rows = joined([b[...] for b in ins])
    for i in range(2):
        copies[2 * i].wait()
        copies[2 * i + 1].wait()
        out_ref[2 * i], out_ref[2 * i + 1] = factors(x_rows, cap, bufs[2 * i], bufs[2 * i + 1])


def unit_grad(blocks, cap, *refs):
    ins, scale_ref = refs[:blocks], refs[blocks]
    weights, outs = refs[blocks + 1 : blocks + 7], refs[blocks + 7 : -7]
    bufs, sems = refs[-7:-1], refs[-1]
    copies = fetch([(weights[i], bufs[i]) for i in (2, 5, 0, 1, 3, 4)], sems)
    grad_rows = joined([b[...] for b in ins])
    lhs = []
    for i in range(2):
        copies[i].wait()
        lhs += hidden_grads(grad_rows, cap, bufs[3 * i + 2], scale_ref[2 * i], scale_ref[2 * i + 1])
    for c in copies[2:]:
        c.wait()
    groups = len(outs) // 2
    input_grads(lhs, [bufs[i] for i in (0, 1, 3, 4)], outs[:groups], outs[groups:])


def add_far(cap, own_ref, far_ref, *out_refs):
    for k, out_ref in enumerate(out_refs):
        part = slice(2 * cap * k, 2 * cap * (k + 1))
        out_ref[...] = (own_ref[part] + far_ref[part].astype(F32)).astype(BF16)


def body(
    x_first,
    grad_first,
    x_second,
    grad_last,
    ids_first,
    probs_first,
    ids_second,
    probs_second,
    w_gate,
    w_up,
    w_down,
):
    tok, width = x_first.shape[1:]
    topk = ids_first.shape[2]
    devices = lax.axis_size("expert")
    sections = lax.axis_size("pipe")
    window = devices // SPLIT
    cap = 3 * tok * topk // (2 * EXPERTS)
    half = width // 2
    shape = jax.ShapeDtypeStruct

    def send(x, bits):
        return lax.ppermute(x, "expert", [(i, i ^ bits) for i in range(devices)])

    def plane(x, k):
        return send(x, SPLIT * k) if k else x

    def across(x):
        return send(x, 2)

    own_w = (w_gate[0, 0], w_up[0, 0], w_down[0, 0])
    msg = shape((2 * cap, half), BF16)
    pair = shape((2, 2 * cap, half), BF16)
    bufs = [pltpu.VMEM(w.shape, BF16) for w in own_w * 2]
    dma = pltpu.SemaphoreType.DMA
    row_buf = pltpu.VMEM((tok, width), BF16)
    order = sequence(window)
    rows = window * 2 * cap
    after = lax.optimization_barrier

    ids_1, probs_1, ids_2, probs_2 = (
        jnp.swapaxes(a[0], 0, 1) for a in (ids_first, probs_first, ids_second, probs_second)
    )
    ring = [(s, (s + 1) % sections) for s in range(sections)]

    def listed(by_k):
        return [by_k[k] for k in order]

    def forward(near, far, *extra):
        return call(
            functools.partial(unit_x, 2 * window, cap),
            shape((4, 2 * rows, w_gate.shape[3]), F32),
            (*listed(near), *listed(far), weights[0], weights[1], weights[3], weights[4], *extra),
            COMPUTE_MIB,
            away=range(2 * window, 2 * window + 4 + len(extra)),
            scratch=[bufs[0], bufs[1], bufs[3], bufs[4], dma((4,))],
            us=2.7,
        )

    groups = [order[:-2], order[-2:]] if window > 2 else [order]
    heights = [2 * cap * len(g) for g in groups]

    def backward(near, far, scales):
        made = call(
            functools.partial(unit_grad, 2 * window, cap),
            [shape((h, half), F32) for h in heights] + [shape((h, half), BF16) for h in heights],
            (*listed(near), *listed(far), scales, *weights),
            COMPUTE_MIB,
            away=range(2 * window + 1, 2 * window + 7),
            scratch=[*bufs, dma((6,))],
            us=5.7,
        )
        back = {}
        for group, own, far in zip(groups, made, made[len(groups) :]):
            far = across(far)
            sums = call(functools.partial(add_far, cap), [msg] * len(group), (own, far), 8)
            back.update({k: plane(sums[j], k) for j, k in enumerate(group)})
        return far, listed(back)

    x_1 = call(
        functools.partial(pack_x, window, cap),
        [msg] * window,
        (ids_1, x_first[0]),
        44,
        away=(1,),
        scratch=[row_buf, dma((4,))],
        us=3.0,
    )
    keys, *packed = call(
        functools.partial(pack_rest, window, cap),
        [shape((2 * topk, tok), F32)] + [msg] * (2 * window),
        (ids_1, probs_1, ids_2, probs_2, grad_first[0], x_second[0], x_1[0]),
        56,
        away=(4, 5, 6),
        scratch=[row_buf, row_buf, dma((8,))],
        us=5.0,
    )
    x_1 = dict(zip(order, x_1))
    grad_1 = dict(zip(order, packed))
    x_2 = dict(zip(order, packed[window:]))
    outer = [k for k in order if k > 1]
    near_x = {k: plane(x_1[k], k) for k in outer}
    peer_w = [send(w, 1) for w in own_w]
    grad_1, peer_w = after((grad_1, peer_w))
    weights = (*own_w, *peer_w)
    near_g = {k: plane(grad_1[k], k) for k in outer}
    inner = [(x_1[k], grad_1[k]) for k in (1, 0)]
    near_x, inner, keys = after((near_x, inner, keys))
    for k, (x, grad) in zip((1, 0), inner):
        near_x[k] = plane(x, k)
        near_g[k] = plane(grad, k)
    far_x = {k: across(near_x[k]) for k in (0, 1, *outer)}
    keys = lax.ppermute(keys, "pipe", ring)
    x_2 = after((near_g, x_2))[1]
    far_g = {k: across(near_g[k]) for k in (0, 1, *outer)}
    near_x2 = {k: plane(x_2[k], k) for k in order}
    arrived, back = backward(near_g, far_g, forward(near_x, far_x))
    near_x2 = after((near_x2, arrived))[0]
    far_x2 = {k: across(near_x2[k]) for k in order}
    scales = forward(near_x2, far_x2)
    dx_first, *grads = call(
        functools.partial(relay, window, cap),
        [shape((1, tok, width), BF16)] + [msg] * window,
        (ids_1, keys, grad_last, *back),
        16,
        away=(2,),
        scratch=[row_buf, dma((4,))],
        us=1.8,
    )
    near = {}
    for j, k in enumerate(order):
        pairs = [
            (s * devices + i, (s - 1) % sections * devices + (i ^ (SPLIT * k)))
            for s in range(sections)
            for i in range(devices)
        ]
        near[k] = lax.ppermute(grads[j], ("pipe", "expert"), pairs)
    far = {k: across(near[k]) for k in order[::-1]}
    _, back = backward(near, far, scales)
    dx_second = call(
        functools.partial(finish, window, cap),
        shape((1, tok, width), BF16),
        (ids_2, *back),
        16,
    )
    return dx_first, dx_second


def solution(mesh):
    split = P("pipe", "expert", None)
    stacked = P("pipe", "expert", None, None)
    return jax.shard_map(
        body,
        mesh=mesh,
        in_specs=(
            split,
            split,
            split,
            P("expert", None),
            split,
            split,
            split,
            split,
            stacked,
            stacked,
            stacked,
        ),
        out_specs=(split, split),
        check_vma=False,
    )
```

```python
import functools

import jax
import jax.numpy as jnp
from jax import lax
from jax.experimental import pallas as pl
from jax.experimental.pallas import tpu as pltpu
from jax.sharding import PartitionSpec as P

EXPERTS = 128
SPLIT = 4
F32, BF16 = jnp.float32, jnp.bfloat16
MIB = 1024 * 1024
COMPUTE_MIB = 26
PACK_MIB = 44


def call(body, outs, args, mib, away=(), scratch=(), us=1.0):
    return pl.pallas_call(
        body,
        out_shape=outs,
        in_specs=[
            pl.BlockSpec(memory_space=pl.ANY if i in away else pltpu.VMEM)
            for i in range(len(args))
        ],
        out_specs=jax.tree.map(lambda _: pl.BlockSpec(memory_space=pltpu.VMEM), outs),
        scratch_shapes=scratch,
        compiler_params=pltpu.CompilerParams(vmem_limit_bytes=mib * MIB),
        cost_estimate=pl.CostEstimate(
            flops=0, bytes_accessed=int(us * 3.6e6), transcendentals=0
        ),
    )(*args)


def fetch(pairs, sems):
    copies = [pltpu.make_async_copy(a, b, sems.at[i]) for i, (a, b) in enumerate(pairs)]
    for c in copies:
        c.start()
    return copies


def row_parts(ref, buf, parts=4):
    step = buf.shape[0] // parts
    return [(ref.at[pl.ds(step * i, step)], buf.at[pl.ds(step * i, step)]) for i in range(parts)]


def sequence(window):
    return [k for k in range(2, window)] + [1, 0][-window:]


def tables(ids_t, window, cap, probs_t=None):
    me = lax.axis_index("expert") // SPLIT
    tok = ids_t.shape[1]
    weights = None
    if probs_t is not None:
        weights = probs_t / jnp.sum(probs_t, axis=0, keepdims=True)
    named, coefs = [], []
    for k in range(window):
        match = ids_t == (me ^ sequence(window)[k])
        named.append(jnp.sum(jnp.where(match, 1.0, 0.0), axis=0, keepdims=True))
        if probs_t is not None:
            coefs.append(jnp.sum(jnp.where(match, weights, 0.0), axis=0, keepdims=True))
    pad = [jnp.zeros((-window % 8, tok), F32)] if window % 8 else []
    stacked = jnp.concatenate(named + pad, axis=0).astype(BF16)
    before = (
        lax.broadcasted_iota(jnp.int32, (tok, tok), 0)
        < lax.broadcasted_iota(jnp.int32, (tok, tok), 1)
    ).astype(F32).astype(BF16)
    place = jnp.dot(stacked, before, preferred_element_type=F32)
    rows = lax.broadcasted_iota(jnp.int32, (2 * cap, tok), 0).astype(F32)
    top, bot, coef = [], [], []
    for k in range(window):
        slot = jnp.where(named[k] > 0.0, place[k : k + 1], -1000.0)
        upper = jnp.where(rows == slot, 1.0, 0.0)
        lower = jnp.where(rows == slot + cap, 1.0, 0.0)
        top.append(upper)
        bot.append(lower)
        if probs_t is not None:
            coef.append(jnp.sum((upper + lower) * coefs[k], axis=1, keepdims=True))
    top, bot = jnp.concatenate(top, axis=0), jnp.concatenate(bot, axis=0)
    return top, bot, jnp.concatenate(coef, axis=0) if coef else None


def gathered(top, bot, rows):
    half = rows.shape[1] // 2
    return jnp.dot(top.astype(BF16), rows[:, :half], preferred_element_type=F32) + jnp.dot(
        bot.astype(BF16), rows[:, half:], preferred_element_type=F32
    )


def pack_x(window, cap, ids_ref, x_ref, *refs):
    out_refs, (x_buf, sems) = refs[-2 - window : -2], refs[-2:]
    copies = fetch(row_parts(x_ref, x_buf), sems)
    top, bot, _ = tables(ids_ref[...], window, cap)
    for c in copies:
        c.wait()
    picked = gathered(top, bot, x_buf[...])
    for k in range(window):
        out_refs[k][...] = picked[2 * cap * k : 2 * cap * (k + 1)].astype(BF16)


def pack_rest(window, cap, ids_ref, probs_ref, ids_on_ref, probs_on_ref, grad_ref, x_ref, *refs):
    out_refs, (grad_buf, x_buf, sems) = refs[-4 - 2 * window : -3], refs[-3:]
    keys_ref, out_refs = out_refs[0], out_refs[1:]
    copies = fetch(row_parts(grad_ref, grad_buf) + row_parts(x_ref, x_buf), sems)
    topk = ids_on_ref.shape[0]
    keys_ref[:topk] = ids_on_ref[...].astype(F32)
    keys_ref[topk:] = probs_on_ref[...]
    top, bot, coef = tables(ids_ref[...], window, cap, probs_ref[...])
    top_on, bot_on, _ = tables(ids_on_ref[...], window, cap)
    for c in copies[:4]:
        c.wait()
    picked = gathered(top, bot, grad_buf[...]) * coef
    for k in range(window):
        out_refs[k][...] = picked[2 * cap * k : 2 * cap * (k + 1)].astype(BF16)
    for c in copies[4:]:
        c.wait()
    picked = gathered(top_on, bot_on, x_buf[...])
    for k in range(window):
        out_refs[window + k][...] = picked[2 * cap * k : 2 * cap * (k + 1)].astype(BF16)


def scattered(ids_ref, window, cap, blocks):
    top, bot, _ = tables(ids_ref[...], window, cap)
    rows = jnp.concatenate([b[...].astype(F32) for b in blocks], axis=0).astype(BF16)
    turned = (((0,), (0,)), ((), ()))
    left = lax.dot_general(top.astype(BF16), rows, turned, preferred_element_type=F32)
    right = lax.dot_general(bot.astype(BF16), rows, turned, preferred_element_type=F32)
    return left.astype(BF16), right.astype(BF16)


def relay(window, cap, ids_ref, keys_ref, grad_last_ref, *refs):
    topk = ids_ref.shape[0]
    blocks, out_refs = refs[:window], refs[window:-2]
    grad_buf, sems = refs[-2:]
    copies = fetch(row_parts(grad_last_ref, grad_buf), sems)
    left, right = scattered(ids_ref, window, cap, blocks)
    half = left.shape[1]
    top, bot, coef = tables(
        keys_ref[:topk].astype(jnp.int32), window, cap, keys_ref[topk:]
    )
    for c in copies:
        c.wait()
    opening = lax.axis_index("pipe") == 0
    left = jnp.where(opening, grad_buf[:, :half], left)
    right = jnp.where(opening, grad_buf[:, half:], right)
    picked = coef * (
        jnp.dot(top.astype(BF16), left, preferred_element_type=F32)
        + jnp.dot(bot.astype(BF16), right, preferred_element_type=F32)
    )
    for k in range(window):
        out_refs[k][...] = picked[2 * cap * k : 2 * cap * (k + 1)].astype(BF16)


def finish(window, cap, ids_ref, *refs):
    blocks, dx_ref = refs[:window], refs[-1]
    left, right = scattered(ids_ref, window, cap, blocks)
    half = left.shape[1]
    dx_ref[0, :, :half] = left
    dx_ref[0, :, half:] = right


NT = (((1,), (1,)), ((), ()))


def joined(blocks):
    return jnp.concatenate([b.astype(F32) for b in blocks], axis=0).astype(BF16)


def factors(rows, cap, gate_ref, up_ref):
    half = rows.shape[1]

    def product(ref):
        lower = jnp.dot(rows, ref[half:, :], preferred_element_type=F32)
        return jnp.dot(rows, ref[:half, :], preferred_element_type=F32) + pltpu.roll(
            lower, rows.shape[0] - cap, 0
        )

    gate, up = product(gate_ref), product(up_ref)
    sig = jax.nn.sigmoid(gate)
    return gate * sig, up * sig * (1.0 + gate * (1.0 - sig))


def hidden_grads(rows, cap, down_ref, for_up, for_gate):
    count, half = rows.shape
    valid = lax.broadcasted_iota(jnp.int32, (count, 1), 0) % (2 * cap) < cap
    lower = lax.dot_general(rows, down_ref[:, half:], NT, preferred_element_type=F32)
    back = lax.dot_general(
        rows, down_ref[:, :half], NT, preferred_element_type=F32
    ) + pltpu.roll(lower, count - cap, 0)
    d_up = jnp.where(valid, back * for_up, 0.0)
    d_gate = jnp.where(valid, back * for_gate, 0.0)
    return [
        (d.astype(BF16), pltpu.roll(d, cap, 0).astype(BF16)) for d in (d_gate, d_up)
    ]


def input_grads(lhs, refs, own_refs, far_refs, step=256):
    half = own_refs[0].shape[1]
    for n in range(0, half, step):
        total = None
        for (upper, lower), ref in zip(lhs, refs):
            term = lax.dot_general(
                upper, ref[n : n + step, :], NT, preferred_element_type=F32
            ) + lax.dot_general(
                lower, ref[half + n : half + n + step, :], NT, preferred_element_type=F32
            )
            total = term if total is None else total + term
        row = 0
        for ref in (*own_refs, *far_refs):
            ref[:, n : n + step] = total[row : row + ref.shape[0]].astype(ref.dtype)
            row += ref.shape[0]


def unit_x(blocks, cap, *refs):
    ins, weights, out_ref, bufs, sems = (
        refs[:blocks],
        refs[blocks : blocks + 4],
        refs[-6],
        refs[-5:-1],
        refs[-1],
    )
    copies = fetch(list(zip(weights, bufs)), sems)
    x_rows = joined([b[...] for b in ins])
    for i in range(2):
        copies[2 * i].wait()
        copies[2 * i + 1].wait()
        out_ref[2 * i], out_ref[2 * i + 1] = factors(x_rows, cap, bufs[2 * i], bufs[2 * i + 1])


def unit_grad(blocks, cap, *refs):
    ins, scale_ref = refs[:blocks], refs[blocks]
    weights, outs = refs[blocks + 1 : blocks + 7], refs[blocks + 7 : -7]
    bufs, sems = refs[-7:-1], refs[-1]
    copies = fetch([(weights[i], bufs[i]) for i in (2, 5, 0, 1, 3, 4)], sems)
    grad_rows = joined([b[...] for b in ins])
    lhs = []
    for i in range(2):
        copies[i].wait()
        lhs += hidden_grads(grad_rows, cap, bufs[3 * i + 2], scale_ref[2 * i], scale_ref[2 * i + 1])
    for c in copies[2:]:
        c.wait()
    groups = len(outs) // 2
    input_grads(lhs, [bufs[i] for i in (0, 1, 3, 4)], outs[:groups], outs[groups:])


def add_far(cap, own_ref, far_ref, *out_refs):
    for k, out_ref in enumerate(out_refs):
        part = slice(2 * cap * k, 2 * cap * (k + 1))
        out_ref[...] = (own_ref[part] + far_ref[part].astype(F32)).astype(BF16)


def body(
    x_first,
    grad_first,
    x_second,
    grad_last,
    ids_first,
    probs_first,
    ids_second,
    probs_second,
    w_gate,
    w_up,
    w_down,
):
    tok, width = x_first.shape[1:]
    topk = ids_first.shape[2]
    devices = lax.axis_size("expert")
    sections = lax.axis_size("pipe")
    window = devices // SPLIT
    cap = 3 * tok * topk // (2 * EXPERTS)
    half = width // 2
    shape = jax.ShapeDtypeStruct

    def send(x, bits):
        return lax.ppermute(x, "expert", [(i, i ^ bits) for i in range(devices)])

    def plane(x, k):
        return send(x, SPLIT * k) if k else x

    def across(x):
        return send(x, 2)

    own_w = (w_gate[0, 0], w_up[0, 0], w_down[0, 0])
    msg = shape((2 * cap, half), BF16)
    pair = shape((2, 2 * cap, half), BF16)
    bufs = [pltpu.VMEM(w.shape, BF16) for w in own_w * 2]
    dma = pltpu.SemaphoreType.DMA
    row_buf = pltpu.VMEM((tok, width), BF16)
    order = sequence(window)
    rows = window * 2 * cap
    after = lax.optimization_barrier

    ids_1, probs_1, ids_2, probs_2 = (
        jnp.swapaxes(a[0], 0, 1) for a in (ids_first, probs_first, ids_second, probs_second)
    )
    ring = [(s, (s + 1) % sections) for s in range(sections)]

    def listed(by_k, ks=order):
        return [by_k[k] for k in ks]

    far_order = order[-2:] + order[:-2]
    x_far_order = order[-2:] + order[:-2]

    def forward(near, far, *extra):
        return call(
            functools.partial(unit_x, 2 * window, cap),
            shape((4, 2 * rows, w_gate.shape[3]), F32),
            (*listed(near), *listed(far, far_order), weights[0], weights[1], weights[3], weights[4], *extra),
            COMPUTE_MIB,
            away=range(2 * window, 2 * window + 4 + len(extra)),
            scratch=[bufs[0], bufs[1], bufs[3], bufs[4], dma((4,))],
            us=2.7,
        )

    groups = [order[:-2], order[-2:]] if window > 2 else [order]
    heights = [2 * cap * len(g) for g in groups]

    def backward(near, far, scales, *held):
        made = call(
            functools.partial(unit_grad, 2 * window, cap),
            [shape((h, half), F32) for h in heights]
            + [shape((h, half), BF16) for h in heights[::-1]],
            (*listed(near), *listed(far, far_order), scales, *weights),
            COMPUTE_MIB,
            away=range(2 * window + 1, 2 * window + 7),
            scratch=[*bufs, dma((6,))],
            us=5.7,
        )
        own, far = made[: len(groups)], list(made[len(groups) :][::-1])
        if held:
            far, held = after((far, *held))
        back = {}
        for group, near_rows, far_rows in zip(groups, own, far):
            far_rows = across(far_rows)
            sums = call(
                functools.partial(add_far, cap), [msg] * len(group), (near_rows, far_rows), 8
            )
            back.update({k: plane(sums[j], k) for j, k in enumerate(group)})
        return far_rows, listed(back), held


    def ended(ids, back, *extra):
        return call(
            functools.partial(finish, window, cap),
            shape((1, tok, width), BF16),
            (ids, *back, *extra),
            16,
            away=range(1 + window, 1 + window + len(extra)),
            us=1.6,
        )

    x_1 = call(
        functools.partial(pack_x, window, cap),
        [msg] * window,
        (ids_1, x_first[0]),
        44,
        away=(1,),
        scratch=[row_buf, dma((4,))],
        us=3.0,
    )
    keys, *packed = call(
        functools.partial(pack_rest, window, cap),
        [shape((2 * topk, tok), F32)] + [msg] * (2 * window),
        (ids_1, probs_1, ids_2, probs_2, grad_first[0], x_second[0], x_1[0]),
        56,
        away=(4, 5, 6),
        scratch=[row_buf, row_buf, dma((8,))],
        us=5.0,
    )
    x_1 = dict(zip(order, x_1))
    grad_1 = dict(zip(order, packed))
    x_2 = dict(zip(order, packed[window:]))
    outer = [k for k in order if k > 1]
    near_x = {k: plane(x_1[k], k) for k in outer}
    peer_w = [send(w, 1) for w in own_w]
    grad_1, peer_w = after((grad_1, peer_w))
    weights = (*own_w, *peer_w)
    near_g = {k: plane(grad_1[k], k) for k in outer}
    near_x[0], near_g[0] = after((x_1[0], grad_1[0]))
    far_x = {0: across(near_x[0])}
    near_x, x_in, grad_in, keys = after((near_x, x_1[1], grad_1[1], keys))
    near_x[1], near_g[1] = plane(x_in, 1), plane(grad_in, 1)
    far_x.update({k: across(near_x[k]) for k in (1, *outer)})
    keys = lax.ppermute(keys, "pipe", ring)
    scales = forward(near_x, far_x)
    x_2 = after((near_g, x_2, scales))[1]
    far_g = {k: across(near_g[k]) for k in (0, 1, *outer)}
    near_x2 = {k: plane(x_2[k], k) for k in order if k > 1}
    arrived, back, near_x2 = backward(near_g, far_g, scales, near_x2)
    near_x2, x_in = after((near_x2, [x_2[1], x_2[0]], arrived))[:2]
    near_x2[1], near_x2[0] = plane(x_in[0], 1), x_in[1]
    far_x2 = {k: across(near_x2[k]) for k in order}
    scales = forward(near_x2, far_x2)
    grads = call(
        functools.partial(relay, window, cap),
        [msg] * window,
        (ids_1, keys, grad_last, *back),
        16,
        away=(2,),
        scratch=[row_buf, dma((4,))],
        us=1.8,
    )
    dx_first = ended(ids_1, back, grads[0])
    near = {}
    for j, k in enumerate(order):
        pairs = [
            (s * devices + i, (s - 1) % sections * devices + (i ^ (SPLIT * k)))
            for s in range(sections)
            for i in range(devices)
        ]
        near[k] = lax.ppermute(grads[j], ("pipe", "expert"), pairs)
    far = {k: across(near[k]) for k in far_order}
    _, back, _ = backward(near, far, scales)
    dx_second = ended(ids_2, back)
    return dx_first, dx_second


def solution(mesh):
    split = P("pipe", "expert", None)
    stacked = P("pipe", "expert", None, None)
    return jax.shard_map(
        body,
        mesh=mesh,
        in_specs=(
            split,
            split,
            split,
            P("expert", None),
            split,
            split,
            split,
            split,
            stacked,
            stacked,
            stacked,
        ),
        out_specs=(split, split),
        check_vma=False,
    )
```
